128 devices in a mesh: section: 4 (over x_hi, core), expert: 32 (over z, y, x_lo).
Axes of the slice: x: 4 (x_hi: 2, x_lo: 2; x = x_hi * 2 + x_lo), y: 4, z: 4, core: 2. Of those that a mesh axis runs over, the one named last changes fastest.
Arguments:
- layer_inputs: bfloat16 [4, 8, 512, 2048], P('section', None, 'expert'), may hold values from -6 to 6
- top_grad: bfloat16 [8, 512, 2048], P('section', 'expert'), may hold values from -6 to 6
- expert_ids: int32 [4, 8, 512, 8], P('section', None, 'expert'), may hold values from 0 to 31, all different within a row; in each aligned block of 16 rows (0 to 15, 16 to 31, ..., all dimensions but the last counted through in order) at most 5 rows name the same one
- router: bfloat16 [4, 2048, 32], P('section'), may hold values from -0.125 to 0.125
- norm_gain: bfloat16 [4, 2048], P('section'), may hold values from 0.099609375 to 1.8984375
- w_gate: bfloat16 [4, 32, 2048, 1024], P('section', 'expert'), may hold values from -0.125 to 0.125
- w_up: bfloat16 [4, 32, 2048, 1024], P('section', 'expert'), may hold values from -0.125 to 0.125
- w_down: bfloat16 [4, 32, 1024, 2048], P('section', 'expert'), may hold values from -0.1875 to 0.1875
Outputs:
- input_grads: bfloat16 [4, 8, 512, 2048], P('section', None, 'expert')
The draws below stay inside these ranges and needn't reach their ends.
Inputs may be any that keep to these rules, and one draw needn't show every extreme that they name: `expert_ids`: each token names 8 different experts. Among the 16 tokens of one device in one micro-batch of one layer, no expert is named by more than 5 of them, and in some of these blocks one expert is named by exactly 5.
All inputs are finite; a program needn't handle non-finite values.
Results may differ from the reference program's by a relative error of at most 0.015.
Values may be sent and summed in bfloat16 or wider, within the bound.
A program may use at most 128 MiB of HBM per device.

```python
import math
import jax
import jax.numpy as jnp
import numpy as np
from jax import lax

D = 2048
FF = 1024
MICRO = 8
TOK_DEV = 16
LAYERS = 4
EXPERTS = 32
TOPK = 8
TOKENS = 512
MOST = 5
N_EXPERT = 32


def steps_of(stream_key, extent, cuts, smallest, top_value):
    level, own = 1.0, jax.random.fold_in(stream_key, 6)
    for axis_at, shards_of in cuts:
        heights = jnp.exp(jax.random.uniform(jax.random.fold_in(own, axis_at), (shards_of,), jnp.float32, smallest / len(cuts), top_value / len(cuts)))
        level = level * jnp.repeat(heights, extent[axis_at] // shards_of).reshape([-1 if axis == axis_at else 1 for axis in range(len(extent))])
    return level


def deal_out(stream_key, own, number, rows, amount, top, reach, skew):
    sequence = jax.random.permutation(stream_key, amount)
    crowded, ordinary = load_shares(amount, rows * top, reach, skew, True), load_shares(amount, rows * top, reach, skew, False)
    places = jnp.arange(amount)

    def named(sizes, rotation):
        used = int((sizes > 0).sum())
        fixed = max(1, used // 4)
        passed = fixed + (places - fixed + rotation * (used - fixed)) % max(1, amount - fixed)
        return jnp.zeros((amount,), jnp.int32).at[sequence[jnp.where(places < fixed, places, passed)]].set(jnp.asarray(sizes, jnp.int32))

    sizes = jnp.where(number % 4 == 0, named(crowded, number // 4), named(ordinary, number - number // 4 - 1))
    mixed = jax.random.permutation(jax.random.fold_in(own, 3), amount)
    giver, sink = mixed[0:amount // 2 * 2:2], mixed[1:amount // 2 * 2:2]
    slack = jnp.minimum(sizes[giver] - 1, reach - sizes[sink]) // 2
    slack = jnp.where((giver == sequence[0]) | (sink == sequence[0]) | (sizes[sink] == 0), 0, jnp.maximum(slack, 0))
    passed = jax.random.randint(jax.random.fold_in(own, 4), (amount // 2,), 0, 1 << 20) % (slack + 1)
    sizes = sizes.at[giver].add(-passed).at[sink].add(passed)
    members = jnp.searchsorted(jnp.cumsum(sizes), jnp.arange(rows * top), side="right").astype(jnp.int32)
    listing = members.reshape(top, rows).T
    listing = listing[jax.random.permutation(jax.random.fold_in(own, 1), rows)]
    rotation = jax.random.randint(jax.random.fold_in(own, 2), (rows, 1), 0, top)
    return jnp.take_along_axis(listing, (jnp.arange(top)[None, :] + rotation) % top, axis=1)


def load_shares(amount, total, most, skew, full):
    portions = [(1 << 20) // math.isqrt(grade ** skew) + 1 for grade in range(1, amount + 1)]
    largest = most if full else min(most, max(-(-total // amount), total * portions[0] // sum(portions)))
    least = 1 if total - largest >= amount - 1 else 0
    counts, spare = [largest] + [least] * (amount - 1), total - largest - least * (amount - 1)
    while spare > 0:
        free = [i for i in range(1, amount) if counts[i] < largest] or [i for i in range(1, amount) if counts[i] < most]
        mass, left = sum([portions[i] for i in free]), spare
        for i in free:
            more = min(most - counts[i], max(1, left * portions[i] // mass), spare)
            counts[i] = counts[i] + more
            spare = spare - more
    return np.array(counts)


def centred(own_key, dims, deviation, most, shards=(), held_as=jnp.bfloat16):
    entries = jax.random.normal(own_key, dims, jnp.float32) * deviation
    if len(shards) > 0:
        entries = steps_of(own_key, dims, shards, -0.22, 0.18) * entries
    return jnp.clip(entries, min=-most, max=most).astype(held_as)


def setup_inputs(seed: int = 0) -> dict:
    key_list = jax.random.split(jax.random.key(seed), 9)
    layer_inputs = centred(key_list[0], (LAYERS, MICRO, TOKENS, D), 1.0, 6.0, ((0, 4), (2, 32)))
    top_grad = centred(key_list[1], (MICRO, TOKENS, D), 1.0, 6.0, ((0, 4), (1, 32)))
    expert_ids_keys = jax.random.split(jax.random.fold_in(key_list[2], 1), LAYERS * MICRO * TOKENS // TOK_DEV)
    expert_ids_turns = jax.random.permutation(jax.random.fold_in(key_list[2], 3), LAYERS * MICRO * TOKENS // TOK_DEV)
    expert_ids = jax.vmap(lambda own, number: deal_out(jax.random.fold_in(key_list[2], 2), own, number, TOK_DEV, N_EXPERT, TOPK, MOST, 2))(expert_ids_keys, expert_ids_turns).reshape((LAYERS, MICRO, TOKENS, TOPK))
    router = centred(key_list[3], (LAYERS, D, EXPERTS), D ** -0.5, 0.125, ((0, 4),))
    norm_gain = jnp.clip(1.0 + 0.18 * jax.random.normal(key_list[4], (LAYERS, D), jnp.float32), 0.099609375, 1.8984375).astype(jnp.bfloat16)
    w_gate = centred(key_list[5], (LAYERS, EXPERTS, D, FF), D ** -0.5, 0.125, ((0, 4), (1, 32)))
    w_up = centred(key_list[6], (LAYERS, EXPERTS, D, FF), D ** -0.5, 0.125, ((0, 4), (1, 32)))
    w_down = centred(key_list[7], (LAYERS, EXPERTS, FF, D), FF ** -0.5, 0.1875, ((0, 4), (1, 32)))
    return dict(layer_inputs=layer_inputs, top_grad=top_grad, expert_ids=expert_ids, router=router, norm_gain=norm_gain, w_gate=w_gate, w_up=w_up, w_down=w_down)


def prepare(x_rows, gain):
    x_float = x_rows.astype(jnp.float32)
    inverse = lax.rsqrt(lax.optimization_barrier(jnp.mean(x_float * x_float, axis=-1, keepdims=True)) + 1e-05)
    normed = (x_float * inverse * gain).astype(jnp.bfloat16)
    return (x_float, inverse, normed)

def expert_rows(normed_rows, grad_rows, gate_w, up_w, down_w):
    gate = jnp.dot(normed_rows, gate_w, preferred_element_type=jnp.float32)
    up_rows = jnp.dot(normed_rows, up_w, preferred_element_type=jnp.float32)
    squash = jax.nn.sigmoid(gate)
    active = gate * squash
    hidden = (active * up_rows).astype(jnp.bfloat16)
    output = jnp.dot(hidden, down_w, preferred_element_type=jnp.float32)
    dprob = lax.optimization_barrier(jnp.sum(output * grad_rows.astype(jnp.float32), axis=-1))
    dhidden = lax.dot_general(grad_rows, down_w, (((1,), (1,)), ((), ())), preferred_element_type=jnp.float32)
    dgate = (dhidden * up_rows * squash * (1.0 + gate * (1.0 - squash))).astype(jnp.bfloat16)
    dup = (dhidden * active).astype(jnp.bfloat16)
    returned = lax.dot_general(dgate, gate_w, (((1,), (1,)), ((), ())), preferred_element_type=jnp.float32)
    returned = returned + lax.dot_general(dup, up_w, (((1,), (1,)), ((), ())), preferred_element_type=jnp.float32)
    return (returned.astype(jnp.bfloat16), dprob)

def finish(x_float, inverse, normed, gain, router_layer, ids, grad_in, pair_back, pair_prob):
    logits = jnp.dot(normed, router_layer, preferred_element_type=jnp.float32)
    raised = jnp.exp(logits)
    probs = raised / lax.optimization_barrier(jnp.sum(raised, axis=-1, keepdims=True))
    choose = (ids[..., None] == jnp.arange(router_layer.shape[1], dtype=jnp.int32)).astype(jnp.float32)
    picked = lax.optimization_barrier(jnp.sum(probs[..., None, :] * choose, axis=-1))
    dfull = lax.optimization_barrier(jnp.sum(pair_prob[..., None] * choose, axis=-2))
    dlogit = probs * (dfull - lax.optimization_barrier(jnp.sum(probs * dfull, axis=-1, keepdims=True)))
    router_term = jnp.dot(dlogit, router_layer.astype(jnp.float32).T, precision=lax.Precision.HIGHEST)
    dnormed = lax.optimization_barrier(jnp.sum(picked[..., None] * pair_back, axis=-2)) + router_term
    scaled = gain * dnormed
    inner = lax.optimization_barrier(jnp.mean(x_float * scaled, axis=-1, keepdims=True))
    result = grad_in.astype(jnp.float32) + inverse * scaled - x_float * inverse * inverse * inverse * inner
    return result.astype(jnp.bfloat16)

def reference(layer_inputs, top_grad, expert_ids, router, norm_gain, w_gate, w_up, w_down):
    pairs = TOPK * TOK_DEV
    total = N_EXPERT * MICRO * N_EXPERT * MOST
    micro_index = jnp.arange(MICRO, dtype=jnp.int32)[:, None, None]
    block_index = jnp.arange(N_EXPERT, dtype=jnp.int32)[None, :, None]
    grad_in = top_grad
    collected = []
    for layer in reversed(range(LAYERS)):
        gain = norm_gain[layer].astype(jnp.float32)
        x_float, inverse, normed = prepare(layer_inputs[layer], gain)
        ids = expert_ids[layer]
        block_ids = ids.reshape(MICRO, N_EXPERT, pairs)
        onehot = (block_ids[..., None] == jnp.arange(N_EXPERT, dtype=jnp.int32)).astype(jnp.int32)
        ranks = lax.optimization_barrier(jnp.sum(onehot * (jnp.cumsum(onehot, axis=2) - 1), axis=-1))
        where = (((block_ids * MICRO + micro_index) * N_EXPERT + block_index) * MOST + ranks).reshape(-1)
        normed_pairs = jnp.repeat(normed, TOPK, axis=1).reshape(-1, D)
        grad_pairs = jnp.repeat(grad_in, TOPK, axis=1).reshape(-1, D)
        normed_buf = jnp.zeros((total, D), jnp.bfloat16).at[where].set(normed_pairs)
        grad_buf = jnp.zeros((total, D), jnp.bfloat16).at[where].set(grad_pairs)
        normed_buf = normed_buf.reshape(N_EXPERT, -1, D)
        grad_buf = grad_buf.reshape(N_EXPERT, -1, D)

        def one_expert(operands):
            return expert_rows(operands[0], operands[1], operands[2], operands[3], operands[4])
        returned, dprob = lax.map(one_expert, (normed_buf, grad_buf, w_gate[layer], w_up[layer], w_down[layer]))
        pair_back = returned.reshape(total, D)[where].astype(jnp.float32).reshape(MICRO, TOKENS, TOPK, D)
        pair_prob = dprob.reshape(total)[where].reshape(MICRO, TOKENS, TOPK)
        result = finish(x_float, inverse, normed, gain, router[layer], ids, grad_in, pair_back, pair_prob)
        collected.append(result)
        grad_in = result
    return jnp.stack(collected[::-1])
```

```python
import jax
import jax.numpy as jnp
from jax import lax
from jax.experimental import pallas as pl
from jax.experimental.pallas import tpu as pltpu
from jax.sharding import PartitionSpec as P

MICRO = 8
TOK = 16
MOST = 5
BLOCKS = 8
LINE = 4
SECTIONS = 4
EXPERTS = 32
GATHERED = BLOCKS * TOK
GROUP = 48
SLOTS = LINE * GROUP
LANES = 128
CONTRACT_LAST = (((1,), (1,)), ((), ()))


def kernel(
    x_ref,
    top_ref,
    sel_ref,
    selt_ref,
    gain_ref,
    router_ref,
    wg_ref,
    wu_ref,
    wd_ref,
    out_ref,
    wcat,
    wdown,
    xn,
    xg,
    dg,
    xr,
    dr,
    rr,
    xs,
    ds,
    cs,
    es,
    ap,
    ac,
    hd,
    pm,
    dcat,
    w_sem,
    xg_s,
    xg_r,
    xr_s,
    xr_r,
    dg_s,
    dg_r,
    dr_s,
    dr_r,
    c_s,
    c_r,
    rr_s,
    rr_r,
    tg_s,
):
    width = x_ref.shape[2]
    inner = wd_ref.shape[0]
    section = lax.axis_index("section")
    me = lax.axis_index("expert")
    z = me // 8
    y = (me // 2) % 4
    x = me % 2
    last = SECTIONS - 1

    def place(k):
        odd = k % 2
        g = z * (1 - odd) + y * odd
        h = y * (1 - odd) + z * odd
        return g, h, 8 - 6 * odd, 2 + 6 * odd

    def rows(start, size):
        return pl.ds(pl.multiple_of(start, 16), size)

    def block_target(k, b):
        _, h, gs, hs = place(k)
        return (b // 2) * gs + h * hs + b % 2

    def my_block(k):
        g, _, _, _ = place(k)
        return g * 2 + x

    def remote(src, dst, ssem, rsem, sec, dev):
        pltpu.make_async_remote_copy(
            src_ref=src,
            dst_ref=dst,
            send_sem=ssem,
            recv_sem=rsem,
            device_id={"section": sec, "expert": dev},
            device_id_type=pl.DeviceIdType.MESH,
        ).start()

    def wait_bytes(ref, sem):
        pltpu.make_async_copy(ref, ref, sem).wait()

    def spread_out(src, k, sec, ssem):
        mine = my_block(k)

        @pl.loop(0, BLOCKS)
        def _(j):
            b = (mine + j) % BLOCKS
            remote(src, dg.at[k, rows(mine * TOK, TOK)], ssem, dg_r.at[k], sec, block_target(k, b))

    def spread_in(src, dst, k, ssem, rsem):
        mine = my_block(k)
        pltpu.make_async_copy(src, dst.at[k, rows(mine * TOK, TOK)], rsem).start()

        @pl.loop(1, BLOCKS)
        def _(j):
            b = (mine + j) % BLOCKS
            remote(src, dst.at[k, rows(mine * TOK, TOK)], ssem, rsem, section, block_target(k, b))

    def along_line(stage, dst, k, ssem, rsem):
        g, h, gs, hs = place(k)
        slot = k % 2
        to = dst.at[k, rows(h * GROUP, GROUP)]
        pltpu.make_async_copy(stage.at[slot, rows(h * GROUP, GROUP)], to, rsem).start()

        @pl.loop(1, LINE)
        def _(j):
            d = (h + j) % LINE
            remote(
                stage.at[slot, rows(d * GROUP, GROUP)], to, ssem, rsem, section, g * gs + d * hs + x
            )

    def pack(src, stage, k):
        slot = k % 2

        @pl.loop(0, width // 512)
        def _(n):
            cols = pl.ds(pl.multiple_of(n * 512, 512), 512)
            stage[slot, :, cols] = jnp.dot(
                sel_ref[k], src[k, :, cols], preferred_element_type=jnp.float32
            ).astype(jnp.bfloat16)

    def inverse_of(xf):
        return lax.rsqrt(jnp.mean(xf * xf, axis=-1, keepdims=True) + 1e-05)

    def send_normed(k):
        xf = x_ref[k].astype(jnp.float32)
        xn[k] = (xf * inverse_of(xf) * gain_ref[...]).astype(jnp.bfloat16)
        spread_in(xn.at[k], xg, k, xg_s.at[k], xg_r.at[k])

    def pack_normed(k):
        wait_bytes(xg.at[k], xg_r.at[k])

        @pl.when(k >= 2)
        def _():
            wait_bytes(xs.at[0, pl.ds(0, SLOTS - GROUP)], xr_s.at[k - 2])

        pack(xg, xs, k)
        along_line(xs, xr, k, xr_s.at[k], xr_r.at[k])

    def forward(k):
        wait_bytes(xr.at[k], xr_r.at[k])
        logits = jnp.dot(
            xr[k], wcat[:, pl.ds(2 * inner, LANES)], preferred_element_type=jnp.float32
        )
        lane = lax.broadcasted_iota(jnp.int32, (SLOTS, LANES), 1)
        raised = jnp.where(lane < EXPERTS, jnp.exp(logits), 0.0)
        probs = raised / jnp.sum(raised, axis=-1, keepdims=True)
        pm[k] = probs
        picked = jnp.sum(jnp.where(lane == me, probs, 0.0), axis=-1, keepdims=True)

        @pl.loop(0, inner // 256)
        def _(n):
            cols = pl.ds(pl.multiple_of(n * 256, 256), 256)
            more = pl.ds(pl.multiple_of(inner + n * 256, 256), 256)
            gate = jnp.dot(xr[k], wcat[:, cols], preferred_element_type=jnp.float32)
            up = jnp.dot(xr[k], wcat[:, more], preferred_element_type=jnp.float32)
            squash = jax.nn.sigmoid(gate)
            active = gate * squash
            hd[k, :, cols] = (active * up).astype(jnp.bfloat16)
            ac[k, :, cols] = (picked * active).astype(jnp.bfloat16)
            ap[k, :, cols] = (picked * up * squash * (1.0 + gate * (1.0 - squash))).astype(
                jnp.bfloat16
            )

    def normed_step(i):
        @pl.when(i < MICRO)
        def _():
            pack_normed(i)

        @pl.when(jnp.logical_and(i >= 1, i <= MICRO))
        def _():
            forward(i - 1)

    def pack_grad(k):
        wait_bytes(dg.at[k], dg_r.at[k])

        @pl.when(k >= 2)
        def _():
            wait_bytes(ds.at[0, pl.ds(0, SLOTS - GROUP)], dr_s.at[k - 2])

        pack(dg, ds, k)
        along_line(ds, dr, k, dr_s.at[k], dr_r.at[k])

    def backward(k):
        wait_bytes(dr.at[k], dr_r.at[k])
        slot = k % 2

        def part(n, dprob):
            cols = pl.ds(pl.multiple_of(n * 256, 256), 256)
            more = pl.ds(pl.multiple_of(inner + n * 256, 256), 256)
            dh = lax.dot_general(
                dr[k], wdown[cols, :], CONTRACT_LAST, preferred_element_type=jnp.float32
            )
            dcat[:, cols] = (dh * ap[k, :, cols].astype(jnp.float32)).astype(jnp.bfloat16)
            dcat[:, more] = (dh * ac[k, :, cols].astype(jnp.float32)).astype(jnp.bfloat16)
            return dprob + jnp.sum(
                dh * hd[k, :, cols].astype(jnp.float32), axis=-1, keepdims=True
            )

        dprob = lax.fori_loop(0, inner // 256, part, jnp.zeros((SLOTS, 1), jnp.float32))
        lane = lax.broadcasted_iota(jnp.int32, (SLOTS, LANES), 1)
        probs = pm[k]
        own = jnp.where(lane == me, 1.0, 0.0)
        picked = jnp.sum(probs * own, axis=-1, keepdims=True)
        dcat[:, pl.ds(2 * inner, LANES)] = (picked * dprob * (own - probs)).astype(jnp.bfloat16)

        @pl.when(k >= 2)
        def _():
            wait_bytes(cs.at[0, pl.ds(0, SLOTS - GROUP)], c_s.at[k - 2])

        @pl.loop(0, width // 256)
        def _(n):
            cols = pl.ds(pl.multiple_of(n * 256, 256), 256)
            cs[slot, :, cols] = lax.dot_general(
                dcat[...], wcat[cols, :], CONTRACT_LAST, preferred_element_type=jnp.float32
            ).astype(jnp.bfloat16)

        along_line(cs, xr, k, c_s.at[k], c_r.at[k])

    def unpack(k):
        wait_bytes(xr.at[k], c_r.at[k])
        slot = k % 2

        @pl.when(k >= 2)
        def _():
            wait_bytes(es.at[0, pl.ds(0, GATHERED - TOK)], rr_s.at[k - 2])

        @pl.loop(0, width // 512)
        def _(n):
            cols = pl.ds(pl.multiple_of(n * 512, 512), 512)
            es[slot, :, cols] = jnp.dot(
                selt_ref[k], xr[k, :, cols], preferred_element_type=jnp.float32
            ).astype(jnp.bfloat16)

        mine = my_block(k)
        to = rr.at[k, rows(mine * TOK, TOK)]
        pltpu.make_async_copy(es.at[slot, rows(mine * TOK, TOK)], to, rr_r.at[k]).start()

        @pl.loop(1, BLOCKS)
        def _(j):
            b = (mine + j) % BLOCKS
            remote(
                es.at[slot, rows(b * TOK, TOK)],
                to,
                rr_s.at[k],
                rr_r.at[k],
                section,
                block_target(k, b),
            )

    def finish(k):
        wait_bytes(rr.at[k], rr_r.at[k])
        dxn = rr[k, pl.ds(0, TOK)].astype(jnp.float32)
        for b in range(1, BLOCKS):
            dxn = dxn + rr[k, pl.ds(b * TOK, TOK)].astype(jnp.float32)
        xf = x_ref[k].astype(jnp.float32)
        inv = inverse_of(xf)
        scaled = gain_ref[...] * dxn
        mean = jnp.mean(xf * scaled, axis=-1, keepdims=True)
        grad = dg[k, rows(my_block(k) * TOK, TOK)].astype(jnp.float32)
        out_ref[k] = (grad + inv * scaled - xf * (inv * inv * inv * mean)).astype(jnp.bfloat16)

        @pl.when(section > 0)
        def _():
            spread_out(out_ref.at[k], k, section - 1, dg_s.at[k])

    weights = [
        pltpu.make_async_copy(wg_ref, wcat.at[:, pl.ds(0, inner)], w_sem.at[0]),
        pltpu.make_async_copy(wu_ref, wcat.at[:, pl.ds(inner, inner)], w_sem.at[1]),
        pltpu.make_async_copy(router_ref, wcat.at[:, pl.ds(2 * inner, LANES)], w_sem.at[2]),
        pltpu.make_async_copy(wd_ref, wdown, w_sem.at[3]),
    ]
    for copy in weights:
        copy.start()

    for half in range(2):
        k = section * 2 + half

        @pl.when(section == last)
        def _():
            spread_in(top_ref.at[half], dg, k, tg_s.at[half], dg_r.at[k])

        @pl.when(section < last)
        def _():
            spread_out(top_ref.at[half], k, last, tg_s.at[half])

    @pl.loop(0, MICRO)
    def _(k):
        send_normed(k)

    for copy in weights:
        copy.wait()

    ahead = jnp.where(section == last, AHEAD_LAST, MICRO)

    @pl.loop(0, ahead + 1)
    def _(i):
        normed_step(i)

    @pl.loop(0, MICRO + 1)
    def _(k):
        @pl.when(k < MICRO)
        def _():
            pack_grad(k)

        @pl.when(k >= 1)
        def _():
            unpack(k - 1)

        normed_step(k + ahead + 1)

        @pl.when(k < MICRO)
        def _():
            backward(k)

        @pl.when(k >= 1)
        def _():
            finish(k - 1)

    @pl.loop(MICRO - 2, MICRO)
    def _(k):
        line = pl.ds(0, SLOTS - GROUP)
        wait_bytes(xs.at[0, line], xr_s.at[k])
        wait_bytes(ds.at[0, line], dr_s.at[k])
        wait_bytes(cs.at[0, line], c_s.at[k])
        wait_bytes(es.at[0, pl.ds(0, GATHERED - TOK)], rr_s.at[k])

    @pl.loop(0, MICRO)
    def _(k):
        wait_bytes(xg.at[0, pl.ds(0, GATHERED - TOK)], xg_s.at[k])

        @pl.when(section > 0)
        def _():
            wait_bytes(dg.at[0], dg_s.at[k])

    for half in range(2):

        @pl.when(section == last)
        def _():
            wait_bytes(dg.at[0, pl.ds(0, GATHERED - TOK)], tg_s.at[half])

        @pl.when(section < last)
        def _():
            wait_bytes(dg.at[0], tg_s.at[half])


AHEAD_LAST = 2


def selections(ids):
    gathered = lax.all_gather(ids, "expert", axis=0).reshape(4, 4, 2, MICRO // 2, 2, TOK, 8)
    me = lax.axis_index("expert")
    z, y, x = me // 8, (me // 2) % 4, me % 2
    even = lax.dynamic_index_in_dim(gathered[:, :, :, :, 0], y, 1, False)
    odd = lax.dynamic_index_in_dim(gathered[:, :, :, :, 1], z, 0, False)
    blocks = jnp.stack([even, odd], axis=3).reshape(BLOCKS, MICRO, TOK, 8)
    blocks = jnp.transpose(blocks, (1, 0, 2, 3))
    line = jnp.arange(LINE, dtype=jnp.int32)
    expert = jnp.stack([z * 8 + line * 2 + x, line * 8 + y * 2 + x])
    expert = jnp.tile(expert, (MICRO // 2, 1))
    named = jnp.any(blocks[:, None] == expert[:, :, None, None, None], axis=-1)
    before = jnp.arange(TOK)[None, :] < jnp.arange(TOK)[:, None]
    rank = jnp.sum((named[:, :, :, None, :] & before).astype(jnp.int32), axis=-1)
    slot = jnp.where(named, rank + MOST * jnp.arange(BLOCKS, dtype=jnp.int32)[:, None], -1)
    slot = slot.reshape(MICRO, LINE, GATHERED)
    group = jnp.arange(GROUP, dtype=jnp.int32)
    sel = (slot[:, :, None, :] == group[:, None]).astype(jnp.bfloat16)
    selt = (jnp.transpose(slot, (0, 2, 1))[..., None] == group).astype(jnp.bfloat16)
    return sel.reshape(MICRO, SLOTS, GATHERED), selt.reshape(MICRO, GATHERED, SLOTS)


def shards(layer_inputs, top_grad, expert_ids, router, norm_gain, w_gate, w_up, w_down):
    width = layer_inputs.shape[3]
    inner = w_down.shape[2]
    sel, selt = selections(expert_ids[0])
    padded = jnp.pad(router[0], ((0, 0), (0, LANES - EXPERTS)))
    vmem = pl.BlockSpec(memory_space=pltpu.VMEM)
    hbm = pl.BlockSpec(memory_space=pl.ANY)
    half = jnp.bfloat16
    line = (MICRO, SLOTS, width)
    gather = (MICRO, GATHERED, width)
    factor = (MICRO, SLOTS, inner)
    dma = pltpu.SemaphoreType.DMA
    out = pl.pallas_call(
        kernel,
        out_shape=jax.ShapeDtypeStruct((MICRO, TOK, width), half),
        in_specs=[vmem] * 5 + [hbm] * 4,
        out_specs=vmem,
        scratch_shapes=[
            pltpu.VMEM((width, 2 * inner + LANES), half),
            pltpu.VMEM((inner, width), half),
            pltpu.VMEM((MICRO, TOK, width), half),
            pltpu.VMEM(gather, half),
            pltpu.VMEM(gather, half),
            pltpu.VMEM(line, half),
            pltpu.VMEM(line, half),
            pltpu.VMEM(gather, half),
            pltpu.VMEM((2, SLOTS, width), half),
            pltpu.VMEM((2, SLOTS, width), half),
            pltpu.VMEM((2, SLOTS, width), half),
            pltpu.VMEM((2, GATHERED, width), half),
            pltpu.VMEM(factor, half),
            pltpu.VMEM(factor, half),
            pltpu.VMEM(factor, half),
            pltpu.VMEM((MICRO, SLOTS, LANES), jnp.float32),
            pltpu.VMEM((SLOTS, 2 * inner + LANES), half),
            dma((4,)),
        ]
        + [dma((MICRO,)) for _ in range(12)]
        + [dma((2,))],
        compiler_params=pltpu.CompilerParams(
            has_side_effects=True, vmem_limit_bytes=60 * 1024 * 1024
        ),
    )(
        layer_inputs[0],
        top_grad,
        sel,
        selt,
        norm_gain.astype(jnp.float32),
        padded,
        w_gate[0, 0],
        w_up[0, 0],
        w_down[0, 0],
    )
    return out[None]


def solution(mesh):
    placed = (
        P("section", None, "expert", None),
        P("section", "expert", None),
        P("section", None, "expert", None),
        P("section", None, None),
        P("section", None),
        P("section", "expert", None, None),
        P("section", "expert", None, None),
        P("section", "expert", None, None),
    )
    return jax.shard_map(
        shards,
        mesh=mesh,
        in_specs=placed,
        out_specs=P("section", None, "expert", None),
        check_vma=False,
    )
```

```python
import jax
import jax.numpy as jnp
from jax import lax
from jax.experimental import pallas as pl
from jax.experimental.pallas import tpu as pltpu
from jax.sharding import PartitionSpec as P

MICRO = 8
TOK = 16
MOST = 5
BLOCKS = 8
LINE = 4
SECTIONS = 4
EXPERTS = 32
GATHERED = BLOCKS * TOK
GROUP = 48
SLOTS = LINE * GROUP
LANES = 128
CONTRACT_LAST = (((1,), (1,)), ((), ()))


def kernel(
    x_ref,
    top_ref,
    ids_ref,
    gain_ref,
    router_ref,
    wg_ref,
    wu_ref,
    wd_ref,
    out_ref,
    wcat,
    wdown,
    xn,
    xg,
    dg,
    xr,
    dr,
    rr,
    xs,
    ds,
    cs,
    es,
    ap,
    ac,
    hd,
    pm,
    dcat,
    sel_ref,
    selt_ref,
    w_sem,
    xg_s,
    xg_r,
    xr_s,
    xr_r,
    dg_s,
    dg_r,
    dr_s,
    dr_r,
    c_s,
    c_r,
    rr_s,
    rr_r,
    tg_s,
):
    width = x_ref.shape[2]
    inner = wd_ref.shape[0]
    section = lax.axis_index("section")
    me = lax.axis_index("expert")
    z = me // 8
    y = (me // 2) % 4
    x = me % 2
    last = SECTIONS - 1

    def place(k):
        odd = k % 2
        g = z * (1 - odd) + y * odd
        h = y * (1 - odd) + z * odd
        return g, h, 8 - 6 * odd, 2 + 6 * odd

    def rows(start, size):
        return pl.ds(pl.multiple_of(start, 16), size)

    def block_target(k, b):
        _, h, gs, hs = place(k)
        return (b // 2) * gs + h * hs + b % 2

    def my_block(k):
        g, _, _, _ = place(k)
        return g * 2 + x

    def remote(src, dst, ssem, rsem, sec, dev):
        pltpu.make_async_remote_copy(
            src_ref=src,
            dst_ref=dst,
            send_sem=ssem,
            recv_sem=rsem,
            device_id={"section": sec, "expert": dev},
            device_id_type=pl.DeviceIdType.MESH,
        ).start()

    def wait_bytes(ref, sem):
        pltpu.make_async_copy(ref, ref, sem).wait()

    def spread_out(src, k, sec, ssem):
        mine = my_block(k)

        @pl.loop(0, BLOCKS)
        def _(j):
            b = (mine + j) % BLOCKS
            remote(src, dg.at[k, rows(mine * TOK, TOK)], ssem, dg_r.at[k], sec, block_target(k, b))

    def spread_in(src, dst, k, ssem, rsem):
        mine = my_block(k)
        pltpu.make_async_copy(src, dst.at[k, rows(mine * TOK, TOK)], rsem).start()

        @pl.loop(1, BLOCKS)
        def _(j):
            b = (mine + j) % BLOCKS
            remote(src, dst.at[k, rows(mine * TOK, TOK)], ssem, rsem, section, block_target(k, b))

    def along_line(stage, dst, k, ssem, rsem):
        g, h, gs, hs = place(k)
        slot = k % 2
        to = dst.at[k, rows(h * GROUP, GROUP)]
        pltpu.make_async_copy(stage.at[slot, rows(h * GROUP, GROUP)], to, rsem).start()

        @pl.loop(1, LINE)
        def _(j):
            d = (h + j) % LINE
            remote(
                stage.at[slot, rows(d * GROUP, GROUP)], to, ssem, rsem, section, g * gs + d * hs + x
            )

    def pack(src, stage, k):
        slot = k % 2

        @pl.loop(0, width // 512)
        def _(n):
            cols = pl.ds(pl.multiple_of(n * 512, 512), 512)
            stage[slot, :, cols] = jnp.dot(
                sel_ref[k], src[k, :, cols], preferred_element_type=jnp.float32
            ).astype(jnp.bfloat16)

    def select(k):
        g, h, gs, hs = place(k)
        named = xg[k, :, pl.ds(width, LANES)]
        here = lax.broadcasted_iota(jnp.int32, (GATHERED, GATHERED), 0)
        other = lax.broadcasted_iota(jnp.int32, (GATHERED, GATHERED), 1)
        before = jnp.logical_and(here // TOK == other // TOK, other < here)
        rank = jnp.dot(
            before.astype(jnp.float32).astype(jnp.bfloat16), named, preferred_element_type=jnp.float32
        )
        block = lax.broadcasted_iota(jnp.int32, (GATHERED, LANES), 0) // TOK
        code = rank + (MOST * block + 1).astype(jnp.float32)
        code = (named.astype(jnp.float32) * code).astype(jnp.bfloat16)
        row = lax.broadcasted_iota(jnp.int32, (SLOTS, LANES), 0)
        lane = lax.broadcasted_iota(jnp.int32, (SLOTS, LANES), 1)
        expert = g * gs + (row // GROUP) * hs + x
        pick = (lane == expert).astype(jnp.float32).astype(jnp.bfloat16)
        held = lax.dot_general(pick, code, CONTRACT_LAST, preferred_element_type=jnp.float32)
        want = (row % GROUP + 1).astype(jnp.float32)
        sel_ref[k] = (held == want).astype(jnp.float32).astype(jnp.bfloat16)
        held = lax.dot_general(code, pick, CONTRACT_LAST, preferred_element_type=jnp.float32)
        want = lax.broadcasted_iota(jnp.int32, (GATHERED, SLOTS), 1) % GROUP + 1
        selt_ref[k] = (held == want.astype(jnp.float32)).astype(jnp.float32).astype(jnp.bfloat16)

    def inverse_of(xf):
        return lax.rsqrt(jnp.mean(xf * xf, axis=-1, keepdims=True) + 1e-05)

    def send_normed(k):
        xf = x_ref[k].astype(jnp.float32)
        xn[k, :, pl.ds(0, width)] = (xf * inverse_of(xf) * gain_ref[...]).astype(jnp.bfloat16)
        ids = ids_ref[k]
        lane = lax.broadcasted_iota(jnp.int32, (TOK, LANES), 1)
        named = jnp.zeros((TOK, LANES), jnp.float32)
        for choice in range(ids.shape[1]):
            named = jnp.where(ids[:, choice : choice + 1] == lane, 1.0, named)
        xn[k, :, pl.ds(width, LANES)] = named.astype(jnp.bfloat16)
        spread_in(xn.at[k], xg, k, xg_s.at[k], xg_r.at[k])

    def pack_normed(k):
        wait_bytes(xg.at[k], xg_r.at[k])

        @pl.when(k >= 2)
        def _():
            wait_bytes(xs.at[0, pl.ds(0, SLOTS - GROUP)], xr_s.at[k - 2])

        select(k)
        pack(xg, xs, k)
        along_line(xs, xr, k, xr_s.at[k], xr_r.at[k])

    def forward(k):
        wait_bytes(xr.at[k], xr_r.at[k])
        logits = jnp.dot(
            xr[k], wcat[:, pl.ds(2 * inner, LANES)], preferred_element_type=jnp.float32
        )
        lane = lax.broadcasted_iota(jnp.int32, (SLOTS, LANES), 1)
        raised = jnp.where(lane < EXPERTS, jnp.exp(logits), 0.0)
        probs = raised / jnp.sum(raised, axis=-1, keepdims=True)
        pm[k] = probs
        picked = jnp.sum(jnp.where(lane == me, probs, 0.0), axis=-1, keepdims=True)

        @pl.loop(0, inner // 256)
        def _(n):
            cols = pl.ds(pl.multiple_of(n * 256, 256), 256)
            more = pl.ds(pl.multiple_of(inner + n * 256, 256), 256)
            gate = jnp.dot(xr[k], wcat[:, cols], preferred_element_type=jnp.float32)
            up = jnp.dot(xr[k], wcat[:, more], preferred_element_type=jnp.float32)
            squash = jax.nn.sigmoid(gate)
            active = gate * squash
            hd[k, :, cols] = (active * up).astype(jnp.bfloat16)
            ac[k, :, cols] = (picked * active).astype(jnp.bfloat16)
            ap[k, :, cols] = (picked * up * squash * (1.0 + gate * (1.0 - squash))).astype(
                jnp.bfloat16
            )

    def normed_step(i):
        @pl.when(i < MICRO)
        def _():
            pack_normed(i)

        @pl.when(jnp.logical_and(i >= 1, i <= MICRO))
        def _():
            forward(i - 1)

    def pack_grad(k):
        wait_bytes(dg.at[k], dg_r.at[k])

        @pl.when(k >= 2)
        def _():
            wait_bytes(ds.at[0, pl.ds(0, SLOTS - GROUP)], dr_s.at[k - 2])

        pack(dg, ds, k)
        along_line(ds, dr, k, dr_s.at[k], dr_r.at[k])

    def backward(k):
        wait_bytes(dr.at[k], dr_r.at[k])
        slot = k % 2

        def part(n, dprob):
            cols = pl.ds(pl.multiple_of(n * 256, 256), 256)
            more = pl.ds(pl.multiple_of(inner + n * 256, 256), 256)
            dh = lax.dot_general(
                dr[k], wdown[cols, :], CONTRACT_LAST, preferred_element_type=jnp.float32
            )
            dcat[:, cols] = (dh * ap[k, :, cols].astype(jnp.float32)).astype(jnp.bfloat16)
            dcat[:, more] = (dh * ac[k, :, cols].astype(jnp.float32)).astype(jnp.bfloat16)
            return dprob + jnp.sum(
                dh * hd[k, :, cols].astype(jnp.float32), axis=-1, keepdims=True
            )

        dprob = lax.fori_loop(0, inner // 256, part, jnp.zeros((SLOTS, 1), jnp.float32))
        lane = lax.broadcasted_iota(jnp.int32, (SLOTS, LANES), 1)
        probs = pm[k]
        own = jnp.where(lane == me, 1.0, 0.0)
        picked = jnp.sum(probs * own, axis=-1, keepdims=True)
        dcat[:, pl.ds(2 * inner, LANES)] = (picked * dprob * (own - probs)).astype(jnp.bfloat16)

        @pl.when(k >= 2)
        def _():
            wait_bytes(cs.at[0, pl.ds(0, SLOTS - GROUP)], c_s.at[k - 2])

        @pl.loop(0, width // 256)
        def _(n):
            cols = pl.ds(pl.multiple_of(n * 256, 256), 256)
            cs[slot, :, cols] = lax.dot_general(
                dcat[...], wcat[cols, :], CONTRACT_LAST, preferred_element_type=jnp.float32
            ).astype(jnp.bfloat16)

        along_line(cs, xr, k, c_s.at[k], c_r.at[k])

    def unpack(k):
        wait_bytes(xr.at[k], c_r.at[k])
        slot = k % 2

        @pl.when(k >= 2)
        def _():
            wait_bytes(es.at[0, pl.ds(0, GATHERED - TOK)], rr_s.at[k - 2])

        @pl.loop(0, width // 512)
        def _(n):
            cols = pl.ds(pl.multiple_of(n * 512, 512), 512)
            es[slot, :, cols] = jnp.dot(
                selt_ref[k], xr[k, :, cols], preferred_element_type=jnp.float32
            ).astype(jnp.bfloat16)

        mine = my_block(k)
        to = rr.at[k, rows(mine * TOK, TOK)]
        pltpu.make_async_copy(es.at[slot, rows(mine * TOK, TOK)], to, rr_r.at[k]).start()

        @pl.loop(1, BLOCKS)
        def _(j):
            b = (mine + j) % BLOCKS
            remote(
                es.at[slot, rows(b * TOK, TOK)],
                to,
                rr_s.at[k],
                rr_r.at[k],
                section,
                block_target(k, b),
            )

    def finish(k):
        wait_bytes(rr.at[k], rr_r.at[k])
        dxn = rr[k, pl.ds(0, TOK)].astype(jnp.float32)
        for b in range(1, BLOCKS):
            dxn = dxn + rr[k, pl.ds(b * TOK, TOK)].astype(jnp.float32)
        xf = x_ref[k].astype(jnp.float32)
        inv = inverse_of(xf)
        scaled = gain_ref[...] * dxn
        mean = jnp.mean(xf * scaled, axis=-1, keepdims=True)
        grad = dg[k, rows(my_block(k) * TOK, TOK)].astype(jnp.float32)
        out_ref[k] = (grad + inv * scaled - xf * (inv * inv * inv * mean)).astype(jnp.bfloat16)

        @pl.when(section > 0)
        def _():
            spread_out(out_ref.at[k], k, section - 1, dg_s.at[k])

    weights = [
        pltpu.make_async_copy(wg_ref, wcat.at[:, pl.ds(0, inner)], w_sem.at[0]),
        pltpu.make_async_copy(wu_ref, wcat.at[:, pl.ds(inner, inner)], w_sem.at[1]),
        pltpu.make_async_copy(router_ref, wcat.at[:, pl.ds(2 * inner, LANES)], w_sem.at[2]),
        pltpu.make_async_copy(wd_ref, wdown, w_sem.at[3]),
    ]
    for copy in weights:
        copy.start()

    for half in range(2):
        k = section * 2 + half

        @pl.when(section == last)
        def _():
            spread_in(top_ref.at[half], dg, k, tg_s.at[half], dg_r.at[k])

        @pl.when(section < last)
        def _():
            spread_out(top_ref.at[half], k, last, tg_s.at[half])

    @pl.loop(0, MICRO)
    def _(k):
        send_normed(k)

    for copy in weights:
        copy.wait()

    ahead = jnp.where(section == last, AHEAD_LAST, MICRO)

    @pl.loop(0, ahead + 1)
    def _(i):
        normed_step(i)

    @pl.loop(0, MICRO + 1)
    def _(k):
        @pl.when(k < MICRO)
        def _():
            pack_grad(k)

        @pl.when(k >= 1)
        def _():
            unpack(k - 1)

        normed_step(k + ahead + 1)

        @pl.when(k < MICRO)
        def _():
            backward(k)

        @pl.when(k >= 1)
        def _():
            finish(k - 1)

    @pl.loop(MICRO - 2, MICRO)
    def _(k):
        line = pl.ds(0, SLOTS - GROUP)
        wait_bytes(xs.at[0, line], xr_s.at[k])
        wait_bytes(ds.at[0, line], dr_s.at[k])
        wait_bytes(cs.at[0, line], c_s.at[k])
        wait_bytes(es.at[0, pl.ds(0, GATHERED - TOK)], rr_s.at[k])

    @pl.loop(0, MICRO)
    def _(k):
        wait_bytes(xg.at[0, pl.ds(0, GATHERED - TOK)], xg_s.at[k])

        @pl.when(section > 0)
        def _():
            wait_bytes(dg.at[0], dg_s.at[k])

    for half in range(2):

        @pl.when(section == last)
        def _():
            wait_bytes(dg.at[0, pl.ds(0, GATHERED - TOK)], tg_s.at[half])

        @pl.when(section < last)
        def _():
            wait_bytes(dg.at[0], tg_s.at[half])


AHEAD_LAST = 2


def shards(layer_inputs, top_grad, expert_ids, router, norm_gain, w_gate, w_up, w_down):
    width = layer_inputs.shape[3]
    inner = w_down.shape[2]
    padded = jnp.pad(router[0], ((0, 0), (0, LANES - EXPERTS)))
    vmem = pl.BlockSpec(memory_space=pltpu.VMEM)
    hbm = pl.BlockSpec(memory_space=pl.ANY)
    half = jnp.bfloat16
    line = (MICRO, SLOTS, width)
    gather = (MICRO, GATHERED, width)
    factor = (MICRO, SLOTS, inner)
    dma = pltpu.SemaphoreType.DMA
    out = pl.pallas_call(
        kernel,
        out_shape=jax.ShapeDtypeStruct((MICRO, TOK, width), half),
        in_specs=[vmem] * 4 + [hbm] * 4,
        out_specs=vmem,
        scratch_shapes=[
            pltpu.VMEM((width, 2 * inner + LANES), half),
            pltpu.VMEM((inner, width), half),
            pltpu.VMEM((MICRO, TOK, width + LANES), half),
            pltpu.VMEM((MICRO, GATHERED, width + LANES), half),
            pltpu.VMEM(gather, half),
            pltpu.VMEM(line, half),
            pltpu.VMEM(line, half),
            pltpu.VMEM(gather, half),
            pltpu.VMEM((2, SLOTS, width), half),
            pltpu.VMEM((2, SLOTS, width), half),
            pltpu.VMEM((2, SLOTS, width), half),
            pltpu.VMEM((2, GATHERED, width), half),
            pltpu.VMEM(factor, half),
            pltpu.VMEM(factor, half),
            pltpu.VMEM(factor, half),
            pltpu.VMEM((MICRO, SLOTS, LANES), jnp.float32),
            pltpu.VMEM((SLOTS, 2 * inner + LANES), half),
            pltpu.VMEM((MICRO, SLOTS, GATHERED), half),
            pltpu.VMEM((MICRO, GATHERED, SLOTS), half),
            dma((4,)),
        ]
        + [dma((MICRO,)) for _ in range(12)]
        + [dma((2,))],
        compiler_params=pltpu.CompilerParams(
            has_side_effects=True, vmem_limit_bytes=60 * 1024 * 1024
        ),
    )(
        layer_inputs[0],
        top_grad,
        expert_ids[0],
        norm_gain.astype(jnp.float32),
        padded,
        w_gate[0, 0],
        w_up[0, 0],
        w_down[0, 0],
    )
    return out[None]


def solution(mesh):
    placed = (
        P("section", None, "expert", None),
        P("section", "expert", None),
        P("section", None, "expert", None),
        P("section", None, None),
        P("section", None),
        P("section", "expert", None, None),
        P("section", "expert", None, None),
        P("section", "expert", None, None),
    )
    return jax.shard_map(
        shards,
        mesh=mesh,
        in_specs=placed,
        out_specs=P("section", None, "expert", None),
        check_vma=False,
    )
```

```python
import jax
import jax.numpy as jnp
from jax import lax
from jax.experimental import pallas as pl
from jax.experimental.pallas import tpu as pltpu
from jax.sharding import PartitionSpec as P

MICRO = 8
TOK = 16
MOST = 5
SECTIONS = 4
EXPERTS = 32
LANES = 128
TILE = 16
SLOTS = EXPERTS * MOST
PART = MOST * TILE
ROWS = SLOTS * TILE
OWN = TOK * TILE
AHEAD_LAST = 2
CONTRACT_LAST = (((1,), (1,)), ((), ()))


def kernel(
    x_ref,
    top_ref,
    ids_ref,
    gain_ref,
    router_ref,
    wg_ref,
    wu_ref,
    wd_ref,
    out_ref,
    wcat,
    wdown,
    swap,
    pick,
    code,
    sel,
    selt,
    dy,
    xr,
    dr,
    xs,
    ds,
    flat,
    ap,
    ac,
    hd,
    pm,
    dcat,
    w_sem,
    xn_s,
    xn_r,
    dy_s,
    dy_r,
    d_s,
    d_r,
    c_s,
    c_r,
    tg_s,
):
    inner, width = wd_ref.shape
    section = lax.axis_index("section")
    me = lax.axis_index("expert")
    last = SECTIONS - 1

    def rows(start, size):
        return pl.ds(pl.multiple_of(start, 16), size)

    def one_hot(mask):
        return mask.astype(jnp.float32).astype(jnp.bfloat16)

    def remote(src, dst, ssem, rsem, sec, dev):
        pltpu.make_async_remote_copy(
            src_ref=src,
            dst_ref=dst,
            send_sem=ssem,
            recv_sem=rsem,
            device_id={"section": sec, "expert": dev},
            device_id_type=pl.DeviceIdType.MESH,
        ).start()

    def wait_bytes(ref, sem):
        pltpu.make_async_copy(ref, ref, sem).wait()

    def exchange(src, dst, ssem, rsem):
        to = dst.at[rows(me * PART, PART)]

        @pl.loop(1, EXPERTS)
        def _(j):
            e = (me + j) % EXPERTS
            remote(src.at[rows(e * PART, PART)], to, ssem, rsem, section, e)

        pltpu.make_async_copy(src.at[rows(me * PART, PART)], to, rsem).start()

    sent = pl.ds(0, ROWS - PART)

    def by_token(values):
        return values.astype(jnp.float32).reshape(TOK, TILE, LANES)

    def mean_of(values):
        return jnp.sum(values, axis=(1, 2), keepdims=True) * (1.0 / width)

    def inverse_of(xf):
        return lax.rsqrt(mean_of(xf * xf) + 1e-05)

    def pack(k, block, stage):
        @pl.loop(0, ROWS // 512)
        def _(n):
            part = rows(n * 512, 512)
            stage[k % 2, part, :] = jnp.dot(
                sel[k, part, :], block, preferred_element_type=jnp.float32
            ).astype(jnp.bfloat16)

    def select(k):
        ids = ids_ref[k]
        lane = lax.broadcasted_iota(jnp.int32, (TOK, LANES), 1)
        named = jnp.zeros((TOK, LANES), jnp.float32)
        for choice in range(ids.shape[1]):
            named = jnp.where(ids[:, choice : choice + 1] == lane, 1.0, named)
        here = lax.broadcasted_iota(jnp.int32, (TOK, TOK), 0)
        other = lax.broadcasted_iota(jnp.int32, (TOK, TOK), 1)
        rank = jnp.dot(
            one_hot(other < here), named.astype(jnp.bfloat16), preferred_element_type=jnp.float32
        )
        first = (named * (TILE * rank + 1.0)).astype(jnp.bfloat16)
        token = lax.broadcasted_iota(jnp.int32, (OWN, TOK), 0) // TILE
        spread = one_hot(token == lax.broadcasted_iota(jnp.int32, (OWN, TOK), 1))
        first = jnp.dot(spread, first, preferred_element_type=jnp.float32)
        offset = lax.broadcasted_iota(jnp.int32, (OWN, LANES), 0) % TILE
        code[k] = jnp.where(first > 0.0, first + offset.astype(jnp.float32), 0.0).astype(
            jnp.bfloat16
        )

        @pl.loop(0, ROWS // 256)
        def _(n):
            part = rows(n * 256, 256)
            held = lax.dot_general(
                pick[part, :], code[k], CONTRACT_LAST, preferred_element_type=jnp.float32
            )
            want = (n * 256 + lax.broadcasted_iota(jnp.int32, (256, OWN), 0)) % PART + 1
            sel[k, part, :] = one_hot(held == want.astype(jnp.float32))

    def select_back(k):
        @pl.loop(0, ROWS // 256)
        def _(n):
            part = pl.ds(pl.multiple_of(n * 256, 256), 256)
            held = lax.dot_general(
                code[k], pick[part, :], CONTRACT_LAST, preferred_element_type=jnp.float32
            )
            want = (n * 256 + lax.broadcasted_iota(jnp.int32, (OWN, 256), 1)) % PART + 1
            selt[k % 2, :, part] = one_hot(held == want.astype(jnp.float32))

    def flatten(tiles, k):
        @pl.loop(0, SLOTS // 16)
        def _(n):
            turned = jnp.dot(
                swap[...], tiles[k, rows(n * 256, 256), :], preferred_element_type=jnp.float32
            ).astype(jnp.bfloat16)
            for j in range(TILE):
                flat[rows(n * 16, 16), pl.ds(j * LANES, LANES)] = turned[j * 16 : (j + 1) * 16]

    def unflatten(tiles, k):
        @pl.loop(0, SLOTS // 16)
        def _(n):
            stacked = jnp.concatenate(
                [flat[rows(n * 16, 16), pl.ds(j * LANES, LANES)] for j in range(TILE)], axis=0
            )
            tiles[k, rows(n * 256, 256), :] = jnp.dot(
                swap[...], stacked, preferred_element_type=jnp.float32
            ).astype(jnp.bfloat16)

    def send_normed(k):
        select(k)

        @pl.when(k >= 2)
        def _():
            wait_bytes(xs.at[0, sent], xn_s.at[k - 2])

        xf = by_token(x_ref[k])
        normed = (xf * inverse_of(xf) * gain_ref[...]).reshape(OWN, LANES).astype(jnp.bfloat16)
        pack(k, normed, xs)
        exchange(xs.at[k % 2], xr.at[k], xn_s.at[k], xn_r.at[k])

    def forward(k):
        wait_bytes(xr.at[k], xn_r.at[k])
        flatten(xr, k)
        logits = jnp.dot(
            flat[...], wcat[:, pl.ds(2 * inner, LANES)], preferred_element_type=jnp.float32
        )
        lane = lax.broadcasted_iota(jnp.int32, (SLOTS, LANES), 1)
        raised = jnp.where(lane < EXPERTS, jnp.exp(logits), 0.0)
        probs = raised / jnp.sum(raised, axis=-1, keepdims=True)
        pm[k] = probs
        picked = jnp.sum(jnp.where(lane == me, probs, 0.0), axis=-1, keepdims=True)

        @pl.loop(0, inner // 256)
        def _(n):
            cols = pl.ds(pl.multiple_of(n * 256, 256), 256)
            more = pl.ds(pl.multiple_of(inner + n * 256, 256), 256)
            gate = jnp.dot(flat[...], wcat[:, cols], preferred_element_type=jnp.float32)
            up = jnp.dot(flat[...], wcat[:, more], preferred_element_type=jnp.float32)
            squash = jax.nn.sigmoid(gate)
            active = gate * squash
            hd[k, :, cols] = (active * up).astype(jnp.bfloat16)
            ac[k, :, cols] = (picked * active).astype(jnp.bfloat16)
            ap[k, :, cols] = (picked * up * squash * (1.0 + gate * (1.0 - squash))).astype(
                jnp.bfloat16
            )

    def normed_step(i):
        @pl.when(i < MICRO)
        def _():
            send_normed(i)

        @pl.when(jnp.logical_and(i >= 1, i <= MICRO))
        def _():
            forward(i - 1)

    def send_grad(k):
        wait_bytes(dy.at[k], dy_r.at[k])

        @pl.when(k >= 2)
        def _():
            wait_bytes(ds.at[0, sent], d_s.at[k - 2])

        pack(k, dy[k], ds)
        exchange(ds.at[k % 2], dr.at[k], d_s.at[k], d_r.at[k])
        select_back(k)

    def backward(k):
        wait_bytes(dr.at[k], d_r.at[k])
        flatten(dr, k)

        def part(n, dprob):
            cols = pl.ds(pl.multiple_of(n * 256, 256), 256)
            more = pl.ds(pl.multiple_of(inner + n * 256, 256), 256)
            dh = lax.dot_general(
                flat[...], wdown[cols, :], CONTRACT_LAST, preferred_element_type=jnp.float32
            )
            dcat[:, cols] = (dh * ap[k, :, cols].astype(jnp.float32)).astype(jnp.bfloat16)
            dcat[:, more] = (dh * ac[k, :, cols].astype(jnp.float32)).astype(jnp.bfloat16)
            return dprob + jnp.sum(
                dh * hd[k, :, cols].astype(jnp.float32), axis=-1, keepdims=True
            )

        dprob = lax.fori_loop(0, inner // 256, part, jnp.zeros((SLOTS, 1), jnp.float32))
        lane = lax.broadcasted_iota(jnp.int32, (SLOTS, LANES), 1)
        probs = pm[k]
        own = jnp.where(lane == me, 1.0, 0.0)
        picked = jnp.sum(probs * own, axis=-1, keepdims=True)
        dcat[:, pl.ds(2 * inner, LANES)] = (picked * dprob * (own - probs)).astype(jnp.bfloat16)

        @pl.loop(0, width // 256)
        def _(n):
            cols = pl.ds(pl.multiple_of(n * 256, 256), 256)
            flat[:, cols] = lax.dot_general(
                dcat[...], wcat[cols, :], CONTRACT_LAST, preferred_element_type=jnp.float32
            ).astype(jnp.bfloat16)

        unflatten(dr, k)
        exchange(dr.at[k], xr.at[k], c_s.at[k], c_r.at[k])

    def finish(k):
        wait_bytes(xr.at[k], c_r.at[k])
        dxn = by_token(jnp.dot(selt[k % 2], xr[k], preferred_element_type=jnp.float32))
        xf = by_token(x_ref[k])
        inv = inverse_of(xf)
        scaled = gain_ref[...] * dxn
        mean = mean_of(xf * scaled)
        grad = by_token(dy[k]) + inv * scaled - xf * (inv * inv * inv * mean)
        out_ref[k] = grad.reshape(OWN, LANES).astype(jnp.bfloat16)

        @pl.when(section > 0)
        def _():
            remote(out_ref.at[k], dy.at[k], dy_s.at[k], dy_r.at[k], section - 1, me)

    for half in range(2):
        at = section * 2 + half

        @pl.when(section == last)
        def _():
            pltpu.make_async_copy(top_ref.at[half], dy.at[at], dy_r.at[at]).start()

        @pl.when(section < last)
        def _():
            remote(top_ref.at[half], dy.at[at], tg_s.at[half], dy_r.at[at], last, me)

    weights = [
        pltpu.make_async_copy(wg_ref, wcat.at[:, pl.ds(0, inner)], w_sem.at[0]),
        pltpu.make_async_copy(wu_ref, wcat.at[:, pl.ds(inner, inner)], w_sem.at[1]),
        pltpu.make_async_copy(router_ref, wcat.at[:, pl.ds(2 * inner, LANES)], w_sem.at[2]),
        pltpu.make_async_copy(wd_ref, wdown, w_sem.at[3]),
    ]
    for copy in weights:
        copy.start()

    here = lax.broadcasted_iota(jnp.int32, (256, 256), 0)
    other = lax.broadcasted_iota(jnp.int32, (256, 256), 1)
    swap[...] = one_hot(
        jnp.logical_and(here % TILE == other // TILE, here // TILE == other % TILE)
    )
    expert = lax.broadcasted_iota(jnp.int32, (ROWS, LANES), 0) // PART
    pick[...] = one_hot(expert == lax.broadcasted_iota(jnp.int32, (ROWS, LANES), 1))
    normed_step(0)
    for copy in weights:
        copy.wait()

    ahead = jnp.where(section == last, AHEAD_LAST, MICRO)

    @pl.loop(1, ahead + 1)
    def _(i):
        normed_step(i)

    @pl.loop(0, MICRO + 1)
    def _(k):
        @pl.when(k < MICRO)
        def _():
            send_grad(k)

        normed_step(k + ahead + 1)

        @pl.when(k >= 1)
        def _():
            finish(k - 1)

        @pl.when(k < MICRO)
        def _():
            backward(k)

    @pl.loop(MICRO - 2, MICRO)
    def _(k):
        wait_bytes(xs.at[0, sent], xn_s.at[k])
        wait_bytes(ds.at[0, sent], d_s.at[k])

    @pl.loop(0, MICRO)
    def _(k):
        wait_bytes(xs.at[0, sent], c_s.at[k])

        @pl.when(section > 0)
        def _():
            wait_bytes(dy.at[0], dy_s.at[k])

    for half in range(2):

        @pl.when(section < last)
        def _():
            wait_bytes(dy.at[0], tg_s.at[half])


def shards(layer_inputs, top_grad, expert_ids, router, norm_gain, w_gate, w_up, w_down):
    width = layer_inputs.shape[3]
    inner = w_down.shape[2]
    padded = jnp.pad(router[0], ((0, 0), (0, LANES - EXPERTS)))
    vmem = pl.BlockSpec(memory_space=pltpu.VMEM)
    hbm = pl.BlockSpec(memory_space=pl.ANY)
    half = jnp.bfloat16
    tiles = (MICRO, ROWS, LANES)
    factor = (MICRO, SLOTS, inner)
    dma = pltpu.SemaphoreType.DMA
    out = pl.pallas_call(
        kernel,
        out_shape=jax.ShapeDtypeStruct((MICRO, OWN, LANES), half),
        in_specs=[vmem] * 4 + [hbm] * 4,
        out_specs=vmem,
        scratch_shapes=[
            pltpu.VMEM((width, 2 * inner + LANES), half),
            pltpu.VMEM((inner, width), half),
            pltpu.VMEM((256, 256), half),
            pltpu.VMEM((ROWS, LANES), half),
            pltpu.VMEM((MICRO, OWN, LANES), half),
            pltpu.VMEM((MICRO, ROWS, OWN), half),
            pltpu.VMEM((2, OWN, ROWS), half),
            pltpu.VMEM((MICRO, OWN, LANES), half),
            pltpu.VMEM(tiles, half),
            pltpu.VMEM(tiles, half),
            pltpu.VMEM((2, ROWS, LANES), half),
            pltpu.VMEM((2, ROWS, LANES), half),
            pltpu.VMEM((SLOTS, width), half),
            pltpu.VMEM(factor, half),
            pltpu.VMEM(factor, half),
            pltpu.VMEM(factor, half),
            pltpu.VMEM((MICRO, SLOTS, LANES), jnp.float32),
            pltpu.VMEM((SLOTS, 2 * inner + LANES), half),
            dma((4,)),
        ]
        + [dma((MICRO,)) for _ in range(8)]
        + [dma((2,))],
        compiler_params=pltpu.CompilerParams(
            has_side_effects=True, vmem_limit_bytes=60 * 1024 * 1024
        ),
    )(
        layer_inputs[0].reshape(MICRO, OWN, LANES),
        top_grad.reshape(2, OWN, LANES),
        expert_ids[0],
        norm_gain.astype(jnp.float32).reshape(1, TILE, LANES),
        padded,
        w_gate[0, 0],
        w_up[0, 0],
        w_down[0, 0],
    )
    return out.reshape(1, MICRO, TOK, width)


def solution(mesh):
    placed = (
        P("section", None, "expert", None),
        P("section", "expert", None),
        P("section", None, "expert", None),
        P("section", None, None),
        P("section", None),
        P("section", "expert", None, None),
        P("section", "expert", None, None),
        P("section", "expert", None, None),
    )
    return jax.shard_map(
        shards,
        mesh=mesh,
        in_specs=placed,
        out_specs=P("section", None, "expert", None),
        check_vma=False,
    )
```

```python
import jax
import jax.numpy as jnp
from jax import lax
from jax.experimental import pallas as pl
from jax.experimental.pallas import tpu as pltpu
from jax.sharding import PartitionSpec as P

MICRO = 8
TOK = 16
MOST = 5
SECTIONS = 4
EXPERTS = 32
LANES = 128
TILE = 16
SLOTS = EXPERTS * MOST
PART = MOST * TILE
ROWS = SLOTS * TILE
OWN = TOK * TILE
CONTRACT_LAST = (((1,), (1,)), ((), ()))


def kernel(
    x_ref,
    top_ref,
    ids_ref,
    gain_ref,
    router_ref,
    wg_ref,
    wu_ref,
    wd_ref,
    out_ref,
    wcat,
    wback,
    wdown,
    swap,
    same,
    xt,
    tt,
    gt,
    pick,
    code,
    sel,
    selt,
    dy,
    xr,
    dr,
    xs,
    ds,
    flat,
    ap,
    ac,
    hd,
    pm,
    dcat,
    w_sem,
    xn_s,
    xn_r,
    dy_s,
    dy_r,
    d_s,
    d_r,
    c_s,
    c_r,
    tg_s,
):
    inner, width = wd_ref.shape
    section = lax.axis_index("section")
    me = lax.axis_index("expert")
    last = SECTIONS - 1

    def rows(start, size):
        return pl.ds(pl.multiple_of(start, 16), size)

    def one_hot(mask):
        return mask.astype(jnp.float32).astype(jnp.bfloat16)

    def remote(src, dst, ssem, rsem, sec, dev):
        pltpu.make_async_remote_copy(
            src_ref=src,
            dst_ref=dst,
            send_sem=ssem,
            recv_sem=rsem,
            device_id={"section": sec, "expert": dev},
            device_id_type=pl.DeviceIdType.MESH,
        ).start()

    def wait_bytes(ref, sem):
        pltpu.make_async_copy(ref, ref, sem).wait()

    def exchange(src, dst, ssem, rsem):
        to = dst.at[rows(me * PART, PART)]

        @pl.loop(1, EXPERTS)
        def _(j):
            e = (me + j) % EXPERTS
            remote(src.at[rows(e * PART, PART)], to, ssem, rsem, section, e)

        pltpu.make_async_copy(src.at[rows(me * PART, PART)], to, rsem).start()

    sent = pl.ds(0, ROWS - PART)

    def tiles_of(pieces):
        return jnp.dot(
            swap[...], jnp.concatenate(pieces, axis=0), preferred_element_type=jnp.float32
        ).astype(jnp.bfloat16)

    def by_token(values):
        return values.astype(jnp.float32).reshape(TOK, TILE, LANES)

    def mean_of(values):
        return jnp.sum(values, axis=(1, 2), keepdims=True) * (1.0 / width)

    def inverse_of(xf):
        return lax.rsqrt(mean_of(xf * xf) + 1e-05)

    def pack(k, block, stage):
        @pl.loop(0, ROWS // 512, unroll=True)
        def _(n):
            part = rows(n * 512, 512)
            stage[k % 2, part, :] = jnp.dot(
                sel[k, part, :], block, preferred_element_type=jnp.float32
            ).astype(jnp.bfloat16)

    def select(k):
        ids = ids_ref[k]
        number = lax.broadcasted_iota(jnp.int32, (LANES, TOK), 0)
        turned = jnp.zeros((LANES, TOK), jnp.float32)
        for choice in range(ids.shape[0]):
            turned = jnp.where(ids[choice : choice + 1, :] == number, 1.0, turned)
        here = lax.broadcasted_iota(jnp.int32, (TOK, TOK), 0)
        other = lax.broadcasted_iota(jnp.int32, (TOK, TOK), 1)
        named = lax.dot_general(
            one_hot(other == here),
            turned.astype(jnp.bfloat16),
            CONTRACT_LAST,
            preferred_element_type=jnp.float32,
        )
        rank = jnp.dot(
            one_hot(other < here), named.astype(jnp.bfloat16), preferred_element_type=jnp.float32
        )
        first = (named * (TILE * rank + 1.0)).astype(jnp.bfloat16)
        token = lax.broadcasted_iota(jnp.int32, (OWN, TOK), 0) // TILE
        spread = one_hot(token == lax.broadcasted_iota(jnp.int32, (OWN, TOK), 1))
        first = jnp.dot(spread, first, preferred_element_type=jnp.float32)
        offset = lax.broadcasted_iota(jnp.int32, (OWN, LANES), 0) % TILE
        found = jnp.where(first > 0.0, first + offset.astype(jnp.float32), 0.0)
        lane = lax.broadcasted_iota(jnp.int32, (OWN, LANES), 1)
        code[k] = jnp.where(lane == EXPERTS, 1.0, found).astype(jnp.bfloat16)

        @pl.loop(0, ROWS // 256, unroll=5)
        def _(n):
            part = rows(n * 256, 256)
            held = lax.dot_general(
                pick[part, :], code[k], CONTRACT_LAST, preferred_element_type=jnp.float32
            )
            sel[k, part, :] = one_hot(held == 0.0)

    def select_back(k):
        @pl.loop(0, ROWS // 256, unroll=5)
        def _(n):
            part = pl.ds(pl.multiple_of(n * 256, 256), 256)
            held = lax.dot_general(
                code[k], pick[part, :], CONTRACT_LAST, preferred_element_type=jnp.float32
            )
            selt[k % 2, :, part] = one_hot(held == 0.0)

    def flatten(tiles, k):
        @pl.loop(0, SLOTS // 16, unroll=5)
        def _(n):
            turned = jnp.dot(
                swap[...], tiles[k, rows(n * 256, 256), :], preferred_element_type=jnp.float32
            ).astype(jnp.bfloat16)
            for j in range(TILE):
                flat[rows(n * 16, 16), pl.ds(j * LANES, LANES)] = turned[j * 16 : (j + 1) * 16]

    def unflatten(tiles, k):
        @pl.loop(0, SLOTS // 16, unroll=5)
        def _(n):
            tiles[k, rows(n * 256, 256), :] = tiles_of(
                [flat[rows(n * 16, 16), pl.ds(j * LANES, LANES)] for j in range(TILE)]
            )

    def send_normed(k):
        select(k)

        @pl.when(k >= 2)
        def _():
            wait_bytes(xs.at[0, sent], xn_s.at[k - 2])

        xt[k] = tiles_of([x_ref[k, :, pl.ds(j * LANES, LANES)] for j in range(TILE)])
        xf = by_token(xt[k])
        normed = (xf * inverse_of(xf) * gt[...][None]).reshape(OWN, LANES).astype(jnp.bfloat16)
        pack(k, normed, xs)
        exchange(xs.at[k % 2], xr.at[k], xn_s.at[k], xn_r.at[k])

    def forward(k):
        wait_bytes(xr.at[k], xn_r.at[k])
        flatten(xr, k)
        logits = lax.dot_general(
            flat[...],
            wback[pl.ds(2 * inner, LANES), :],
            CONTRACT_LAST,
            preferred_element_type=jnp.float32,
        )
        lane = lax.broadcasted_iota(jnp.int32, (SLOTS, LANES), 1)
        raised = jnp.where(lane < EXPERTS, jnp.exp(logits), 0.0)
        probs = raised / jnp.sum(raised, axis=-1, keepdims=True)
        pm[k] = probs
        picked = jnp.sum(jnp.where(lane == me, probs, 0.0), axis=-1, keepdims=True)

        @pl.loop(0, inner // 256)
        def _(n):
            cols = pl.ds(pl.multiple_of(n * 256, 256), 256)
            more = pl.ds(pl.multiple_of(inner + n * 256, 256), 256)
            gate = jnp.dot(flat[...], wcat[:, cols], preferred_element_type=jnp.float32)
            up = jnp.dot(flat[...], wcat[:, more], preferred_element_type=jnp.float32)
            squash = jax.nn.sigmoid(gate)
            active = gate * squash
            hd[k, :, cols] = (active * up).astype(jnp.bfloat16)
            ac[k, :, cols] = (picked * active).astype(jnp.bfloat16)
            ap[k, :, cols] = (picked * up * squash * (1.0 + gate * (1.0 - squash))).astype(
                jnp.bfloat16
            )

    def normed_step(i):
        @pl.when(i < MICRO)
        def _():
            send_normed(i)

        @pl.when(jnp.logical_and(i >= 1, i <= MICRO))
        def _():
            forward(i - 1)

    def send_grad(k):
        wait_bytes(dy.at[k], dy_r.at[k])

        @pl.when(k >= 2)
        def _():
            wait_bytes(ds.at[0, sent], d_s.at[k - 2])

        pack(k, dy[k], ds)
        exchange(ds.at[k % 2], dr.at[k], d_s.at[k], d_r.at[k])
        select_back(k)

    def backward(k):
        wait_bytes(dr.at[k], d_r.at[k])
        flatten(dr, k)

        def part(n, dprob):
            cols = pl.ds(pl.multiple_of(n * 256, 256), 256)
            more = pl.ds(pl.multiple_of(inner + n * 256, 256), 256)
            dh = jnp.dot(flat[...], wdown[:, cols], preferred_element_type=jnp.float32)
            dcat[:, cols] = (dh * ap[k, :, cols].astype(jnp.float32)).astype(jnp.bfloat16)
            dcat[:, more] = (dh * ac[k, :, cols].astype(jnp.float32)).astype(jnp.bfloat16)
            return dprob + jnp.sum(
                dh * hd[k, :, cols].astype(jnp.float32), axis=-1, keepdims=True
            )

        dprob = lax.fori_loop(0, inner // 256, part, jnp.zeros((SLOTS, 1), jnp.float32))
        lane = lax.broadcasted_iota(jnp.int32, (SLOTS, LANES), 1)
        probs = pm[k]
        own = jnp.where(lane == me, 1.0, 0.0)
        picked = jnp.sum(probs * own, axis=-1, keepdims=True)
        dcat[:, pl.ds(2 * inner, LANES)] = (picked * dprob * (own - probs)).astype(jnp.bfloat16)

        @pl.loop(0, width // 256)
        def _(n):
            cols = pl.ds(pl.multiple_of(n * 256, 256), 256)
            flat[:, cols] = jnp.dot(
                dcat[...], wback[:, cols], preferred_element_type=jnp.float32
            ).astype(jnp.bfloat16)

        unflatten(dr, k)
        exchange(dr.at[k], xr.at[k], c_s.at[k], c_r.at[k])

    def finish(k):
        wait_bytes(xr.at[k], c_r.at[k])
        dxn = by_token(jnp.dot(selt[k % 2], xr[k], preferred_element_type=jnp.float32))
        xf = by_token(xt[k])
        inv = inverse_of(xf)
        scaled = gt[...][None] * dxn
        mean = mean_of(xf * scaled)
        grad = by_token(dy[k]) + inv * scaled - xf * (inv * inv * inv * mean)
        out_ref[k] = grad.reshape(OWN, LANES).astype(jnp.bfloat16)

        @pl.when(section > 0)
        def _():
            remote(out_ref.at[k], dy.at[k], dy_s.at[k], dy_r.at[k], section - 1, me)

    def turn_weights():
        @pl.loop(0, inner // 256)
        def _(n):
            part = pl.ds(pl.multiple_of(n * 256, 256), 256)
            for m in range(width // 256):
                other = pl.ds(m * 256, 256)
                wdown[other, part] = lax.dot_general(
                    same[...], wback[part, other], CONTRACT_LAST, preferred_element_type=jnp.float32
                ).astype(jnp.bfloat16)

        @pl.loop(0, 2 * inner // 256)
        def _(n):
            part = pl.ds(pl.multiple_of(n * 256, 256), 256)
            for m in range(width // 256):
                other = pl.ds(m * 256, 256)
                wback[part, other] = lax.dot_general(
                    same[...], wcat[other, part], CONTRACT_LAST, preferred_element_type=jnp.float32
                ).astype(jnp.bfloat16)

    weights = [
        pltpu.make_async_copy(wg_ref, wcat.at[:, pl.ds(0, inner)], w_sem.at[0]),
        pltpu.make_async_copy(wu_ref, wcat.at[:, pl.ds(inner, inner)], w_sem.at[1]),
        pltpu.make_async_copy(wd_ref, wback.at[pl.ds(0, inner), :], w_sem.at[2]),
    ]
    for copy in weights:
        copy.start()

    here = lax.broadcasted_iota(jnp.int32, (256, 256), 0)
    other = lax.broadcasted_iota(jnp.int32, (256, 256), 1)
    swap[...] = one_hot(
        jnp.logical_and(here % TILE == other // TILE, here // TILE == other % TILE)
    )
    same[...] = one_hot(here == other)
    for half in range(2):
        at = section * 2 + half
        tt[half] = tiles_of([top_ref[half, :, pl.ds(j * LANES, LANES)] for j in range(TILE)])

        @pl.when(section == last)
        def _():
            pltpu.make_async_copy(tt.at[half], dy.at[at], dy_r.at[at]).start()

        @pl.when(section < last)
        def _():
            remote(tt.at[half], dy.at[at], tg_s.at[half], dy_r.at[at], last, me)

    wback[pl.ds(2 * inner, EXPERTS), :] = router_ref[...]
    wback[pl.ds(2 * inner + EXPERTS, LANES - EXPERTS), :] = jnp.zeros(
        (LANES - EXPERTS, width), jnp.bfloat16
    )
    for j in range(TILE):
        gt[pl.ds(j, 1), :] = gain_ref[:, pl.ds(j * LANES, LANES)].astype(jnp.float32)
    for e in range(EXPERTS):
        lane = lax.broadcasted_iota(jnp.int32, (PART, LANES), 1)
        place = lax.broadcasted_iota(jnp.int32, (PART, LANES), 0).astype(jnp.float32)
        pick[pl.ds(e * PART, PART), :] = jnp.where(
            lane == EXPERTS, -1.0 - place, jnp.where(lane == e, 1.0, 0.0)
        ).astype(jnp.bfloat16)
    ahead = jnp.where(section == last, 1, jnp.where(section == last - 1, 3, MICRO))

    @pl.loop(0, ahead + 1)
    def _(i):
        normed_step(i)

        @pl.when(i == 0)
        def _():
            for copy in weights:
                copy.wait()
            turn_weights()

    @pl.loop(0, MICRO + 1)
    def _(k):
        @pl.when(k < MICRO)
        def _():
            send_grad(k)

        @pl.when(k >= 1)
        def _():
            finish(k - 1)

        normed_step(k + ahead + 1)

        @pl.when(k < MICRO)
        def _():
            backward(k)

    @pl.loop(MICRO - 2, MICRO)
    def _(k):
        wait_bytes(xs.at[0, sent], xn_s.at[k])
        wait_bytes(ds.at[0, sent], d_s.at[k])

    @pl.loop(0, MICRO)
    def _(k):
        wait_bytes(xs.at[0, sent], c_s.at[k])

        @pl.when(section > 0)
        def _():
            wait_bytes(dy.at[0], dy_s.at[k])

    for half in range(2):

        @pl.when(section < last)
        def _():
            wait_bytes(dy.at[0], tg_s.at[half])


def shards(layer_inputs, top_grad, expert_ids, router, norm_gain, w_gate, w_up, w_down):
    width = layer_inputs.shape[3]
    inner = w_down.shape[2]
    vmem = pl.BlockSpec(memory_space=pltpu.VMEM)
    hbm = pl.BlockSpec(memory_space=pl.ANY)
    half = jnp.bfloat16
    tiles = (MICRO, ROWS, LANES)
    factor = (MICRO, SLOTS, inner)
    dma = pltpu.SemaphoreType.DMA
    out = pl.pallas_call(
        kernel,
        out_shape=jax.ShapeDtypeStruct((MICRO, OWN, LANES), half),
        in_specs=[vmem] * 5 + [hbm] * 3,
        out_specs=vmem,
        scratch_shapes=[
            pltpu.VMEM((width, 2 * inner), half),
            pltpu.VMEM((2 * inner + LANES, width), half),
            pltpu.VMEM((width, inner), half),
            pltpu.VMEM((256, 256), half),
            pltpu.VMEM((256, 256), half),
            pltpu.VMEM((MICRO, OWN, LANES), half),
            pltpu.VMEM((2, OWN, LANES), half),
            pltpu.VMEM((TILE, LANES), jnp.float32),
            pltpu.VMEM((ROWS, LANES), half),
            pltpu.VMEM((MICRO, OWN, LANES), half),
            pltpu.VMEM((MICRO, ROWS, OWN), half),
            pltpu.VMEM((2, OWN, ROWS), half),
            pltpu.VMEM((MICRO, OWN, LANES), half),
            pltpu.VMEM(tiles, half),
            pltpu.VMEM(tiles, half),
            pltpu.VMEM((2, ROWS, LANES), half),
            pltpu.VMEM((2, ROWS, LANES), half),
            pltpu.VMEM((SLOTS, width), half),
            pltpu.VMEM(factor, half),
            pltpu.VMEM(factor, half),
            pltpu.VMEM(factor, half),
            pltpu.VMEM((MICRO, SLOTS, LANES), jnp.float32),
            pltpu.VMEM((SLOTS, 2 * inner + LANES), half),
            dma((3,)),
        ]
        + [dma((MICRO,)) for _ in range(8)]
        + [dma((2,))],
        compiler_params=pltpu.CompilerParams(
            has_side_effects=True, vmem_limit_bytes=60 * 1024 * 1024
        ),
    )(
        layer_inputs[0],
        top_grad,
        jnp.transpose(expert_ids[0], (0, 2, 1)),
        norm_gain,
        jnp.transpose(router[0]),
        w_gate[0, 0],
        w_up[0, 0],
        w_down[0, 0],
    )
    return out.reshape(1, MICRO, TOK, width)


def solution(mesh):
    placed = (
        P("section", None, "expert", None),
        P("section", "expert", None),
        P("section", None, "expert", None),
        P("section", None, None),
        P("section", None),
        P("section", "expert", None, None),
        P("section", "expert", None, None),
        P("section", "expert", None, None),
    )
    return jax.shard_map(
        shards,
        mesh=mesh,
        in_specs=placed,
        out_specs=P("section", None, "expert", None),
        check_vma=False,
    )
```

```python
import jax
import jax.numpy as jnp
from jax import lax
from jax.experimental import pallas as pl
from jax.experimental.pallas import tpu as pltpu
from jax.sharding import PartitionSpec as P

MICRO = 8
TOK = 16
MOST = 5
SECTIONS = 4
EXPERTS = 32
LANES = 128
TILE = 16
SLOTS = EXPERTS * MOST
PART = MOST * TILE
ROWS = SLOTS * TILE
OWN = TOK * TILE
CONTRACT_LAST = (((1,), (1,)), ((), ()))


def kernel(
    x_ref,
    top_ref,
    ids_ref,
    gain_ref,
    router_ref,
    wg_ref,
    wu_ref,
    wd_ref,
    out_ref,
    wcat,
    wback,
    wdown,
    swap,
    same,
    xt,
    tt,
    gt,
    pick,
    code,
    sel,
    selt,
    dy,
    xr,
    dr,
    xs,
    ds,
    flat,
    ap,
    ac,
    hd,
    pm,
    dcat,
    w_sem,
    xn_s,
    xn_r,
    dy_s,
    dy_r,
    d_s,
    d_r,
    c_s,
    c_r,
    tg_s,
):
    inner, width = wd_ref.shape
    section = lax.axis_index("section")
    me = lax.axis_index("expert")
    last = SECTIONS - 1

    def rows(start, size):
        return pl.ds(pl.multiple_of(start, 16), size)

    def one_hot(mask):
        return mask.astype(jnp.float32).astype(jnp.bfloat16)

    def remote(src, dst, ssem, rsem, sec, dev):
        pltpu.make_async_remote_copy(
            src_ref=src,
            dst_ref=dst,
            send_sem=ssem,
            recv_sem=rsem,
            device_id={"section": sec, "expert": dev},
            device_id_type=pl.DeviceIdType.MESH,
        ).start()

    def wait_bytes(ref, sem):
        pltpu.make_async_copy(ref, ref, sem).wait()

    def exchange(src, dst, ssem, rsem):
        to = dst.at[rows(me * PART, PART)]

        @pl.loop(1, EXPERTS)
        def _(j):
            e = (me + j) % EXPERTS
            remote(src.at[rows(e * PART, PART)], to, ssem, rsem, section, e)

        pltpu.make_async_copy(src.at[rows(me * PART, PART)], to, rsem).start()

    sent = pl.ds(0, ROWS - PART)

    def tiles_of(pieces):
        return jnp.dot(
            swap[...], jnp.concatenate(pieces, axis=0), preferred_element_type=jnp.float32
        ).astype(jnp.bfloat16)

    def by_token(values):
        return values.astype(jnp.float32).reshape(TOK, TILE, LANES)

    def mean_of(values):
        return jnp.sum(values, axis=(1, 2), keepdims=True) * (1.0 / width)

    def inverse_of(xf):
        return lax.rsqrt(mean_of(xf * xf) + 1e-05)

    def pack(k, block, stage):
        @pl.loop(0, ROWS // 512, unroll=True)
        def _(n):
            part = rows(n * 512, 512)
            stage[k % 2, part, :] = jnp.dot(
                sel[k, part, :], block, preferred_element_type=jnp.float32
            ).astype(jnp.bfloat16)

    def select(k):
        ids = ids_ref[k]
        number = lax.broadcasted_iota(jnp.int32, (LANES, TOK), 0)
        turned = jnp.zeros((LANES, TOK), jnp.float32)
        for choice in range(ids.shape[0]):
            turned = jnp.where(ids[choice : choice + 1, :] == number, 1.0, turned)
        here = lax.broadcasted_iota(jnp.int32, (TOK, TOK), 0)
        other = lax.broadcasted_iota(jnp.int32, (TOK, TOK), 1)
        named = lax.dot_general(
            one_hot(other == here),
            turned.astype(jnp.bfloat16),
            CONTRACT_LAST,
            preferred_element_type=jnp.float32,
        )
        rank = jnp.dot(
            one_hot(other < here), named.astype(jnp.bfloat16), preferred_element_type=jnp.float32
        )
        first = (named * (TILE * rank + 1.0)).astype(jnp.bfloat16)
        token = lax.broadcasted_iota(jnp.int32, (OWN, TOK), 0) // TILE
        spread = one_hot(token == lax.broadcasted_iota(jnp.int32, (OWN, TOK), 1))
        first = jnp.dot(spread, first, preferred_element_type=jnp.float32)
        offset = lax.broadcasted_iota(jnp.int32, (OWN, LANES), 0) % TILE
        found = jnp.where(first > 0.0, first + offset.astype(jnp.float32), 0.0)
        lane = lax.broadcasted_iota(jnp.int32, (OWN, LANES), 1)
        code[k] = jnp.where(lane == EXPERTS, 1.0, found).astype(jnp.bfloat16)

        @pl.loop(0, ROWS // 256, unroll=5)
        def _(n):
            part = rows(n * 256, 256)
            held = lax.dot_general(
                pick[part, :], code[k], CONTRACT_LAST, preferred_element_type=jnp.float32
            )
            sel[k, part, :] = one_hot(held == 0.0)

    def select_back(k):
        @pl.loop(0, ROWS // 256, unroll=5)
        def _(n):
            part = pl.ds(pl.multiple_of(n * 256, 256), 256)
            held = lax.dot_general(
                code[k], pick[part, :], CONTRACT_LAST, preferred_element_type=jnp.float32
            )
            selt[k % 2, :, part] = one_hot(held == 0.0)

    def flatten(tiles, k):
        @pl.loop(0, SLOTS // 16, unroll=5)
        def _(n):
            turned = jnp.dot(
                swap[...], tiles[k, rows(n * 256, 256), :], preferred_element_type=jnp.float32
            ).astype(jnp.bfloat16)
            for j in range(TILE):
                flat[rows(n * 16, 16), pl.ds(j * LANES, LANES)] = turned[j * 16 : (j + 1) * 16]

    def unflatten(tiles, k):
        @pl.loop(0, SLOTS // 16, unroll=5)
        def _(n):
            tiles[k, rows(n * 256, 256), :] = tiles_of(
                [flat[rows(n * 16, 16), pl.ds(j * LANES, LANES)] for j in range(TILE)]
            )

    def send_normed(k):
        select(k)

        @pl.when(k >= 2)
        def _():
            wait_bytes(xs.at[0, sent], xn_s.at[k - 2])

        xt[k] = tiles_of([x_ref[k, :, pl.ds(j * LANES, LANES)] for j in range(TILE)])
        xf = by_token(xt[k])
        normed = (xf * inverse_of(xf) * gt[...][None]).reshape(OWN, LANES).astype(jnp.bfloat16)
        pack(k, normed, xs)
        exchange(xs.at[k % 2], xr.at[k], xn_s.at[k], xn_r.at[k])

    def forward(k):
        wait_bytes(xr.at[k], xn_r.at[k])
        flatten(xr, k)
        logits = lax.dot_general(
            flat[...],
            wback[pl.ds(2 * inner, LANES), :],
            CONTRACT_LAST,
            preferred_element_type=jnp.float32,
        )
        lane = lax.broadcasted_iota(jnp.int32, (SLOTS, LANES), 1)
        raised = jnp.where(lane < EXPERTS, jnp.exp(logits), 0.0)
        probs = raised / jnp.sum(raised, axis=-1, keepdims=True)
        pm[k] = probs
        picked = jnp.sum(jnp.where(lane == me, probs, 0.0), axis=-1, keepdims=True)

        @pl.loop(0, inner // 256)
        def _(n):
            cols = pl.ds(pl.multiple_of(n * 256, 256), 256)
            more = pl.ds(pl.multiple_of(inner + n * 256, 256), 256)
            gate = jnp.dot(flat[...], wcat[:, cols], preferred_element_type=jnp.float32)
            up = jnp.dot(flat[...], wcat[:, more], preferred_element_type=jnp.float32)
            squash = jax.nn.sigmoid(gate)
            active = gate * squash
            hd[k, :, cols] = (active * up).astype(jnp.bfloat16)
            ac[k, :, cols] = (picked * active).astype(jnp.bfloat16)
            ap[k, :, cols] = (picked * up * squash * (1.0 + gate * (1.0 - squash))).astype(
                jnp.bfloat16
            )

    def normed_step(i):
        @pl.when(i < MICRO)
        def _():
            send_normed(i)

        @pl.when(jnp.logical_and(i >= 1, i <= MICRO))
        def _():
            forward(i - 1)

    def send_grad(k):
        wait_bytes(dy.at[k], dy_r.at[k])

        @pl.when(k >= 2)
        def _():
            wait_bytes(ds.at[0, sent], d_s.at[k - 2])

        pack(k, dy[k], ds)
        exchange(ds.at[k % 2], dr.at[k], d_s.at[k], d_r.at[k])
        select_back(k)

    def backward(k):
        wait_bytes(dr.at[k], d_r.at[k])
        flatten(dr, k)

        def part(n, dprob):
            cols = pl.ds(pl.multiple_of(n * 256, 256), 256)
            more = pl.ds(pl.multiple_of(inner + n * 256, 256), 256)
            dh = jnp.dot(flat[...], wdown[:, cols], preferred_element_type=jnp.float32)
            dcat[:, cols] = (dh * ap[k, :, cols].astype(jnp.float32)).astype(jnp.bfloat16)
            dcat[:, more] = (dh * ac[k, :, cols].astype(jnp.float32)).astype(jnp.bfloat16)
            return dprob + jnp.sum(
                dh * hd[k, :, cols].astype(jnp.float32), axis=-1, keepdims=True
            )

        dprob = lax.fori_loop(0, inner // 256, part, jnp.zeros((SLOTS, 1), jnp.float32))
        lane = lax.broadcasted_iota(jnp.int32, (SLOTS, LANES), 1)
        probs = pm[k]
        own = jnp.where(lane == me, 1.0, 0.0)
        picked = jnp.sum(probs * own, axis=-1, keepdims=True)
        dcat[:, pl.ds(2 * inner, LANES)] = (picked * dprob * (own - probs)).astype(jnp.bfloat16)

        @pl.loop(0, width // 256)
        def _(n):
            cols = pl.ds(pl.multiple_of(n * 256, 256), 256)
            flat[:, cols] = jnp.dot(
                dcat[...], wback[:, cols], preferred_element_type=jnp.float32
            ).astype(jnp.bfloat16)

        unflatten(dr, k)
        exchange(dr.at[k], xr.at[k], c_s.at[k], c_r.at[k])

    def finish(k):
        wait_bytes(xr.at[k], c_r.at[k])
        dxn = by_token(jnp.dot(selt[k % 2], xr[k], preferred_element_type=jnp.float32))
        xf = by_token(xt[k])
        inv = inverse_of(xf)
        scaled = gt[...][None] * dxn
        mean = mean_of(xf * scaled)
        grad = by_token(dy[k]) + inv * scaled - xf * (inv * inv * inv * mean)
        out_ref[k] = grad.reshape(OWN, LANES).astype(jnp.bfloat16)

        @pl.when(section > 0)
        def _():
            remote(out_ref.at[k], dy.at[k], dy_s.at[k], dy_r.at[k], section - 1, me)

    def turn_weights():
        @pl.loop(0, inner // 256)
        def _(n):
            part = pl.ds(pl.multiple_of(n * 256, 256), 256)
            for m in range(width // 256):
                other = pl.ds(m * 256, 256)
                wdown[other, part] = lax.dot_general(
                    same[...], wback[part, other], CONTRACT_LAST, preferred_element_type=jnp.float32
                ).astype(jnp.bfloat16)

        @pl.loop(0, 2 * inner // 256)
        def _(n):
            part = pl.ds(pl.multiple_of(n * 256, 256), 256)
            for m in range(width // 256):
                other = pl.ds(m * 256, 256)
                wback[part, other] = lax.dot_general(
                    same[...], wcat[other, part], CONTRACT_LAST, preferred_element_type=jnp.float32
                ).astype(jnp.bfloat16)

    weights = [
        pltpu.make_async_copy(wg_ref, wcat.at[:, pl.ds(0, inner)], w_sem.at[0]),
        pltpu.make_async_copy(wu_ref, wcat.at[:, pl.ds(inner, inner)], w_sem.at[1]),
        pltpu.make_async_copy(wd_ref, wback.at[pl.ds(0, inner), :], w_sem.at[2]),
    ]
    for copy in weights:
        copy.start()

    here = lax.broadcasted_iota(jnp.int32, (256, 256), 0)
    other = lax.broadcasted_iota(jnp.int32, (256, 256), 1)
    swap[...] = one_hot(
        jnp.logical_and(here % TILE == other // TILE, here // TILE == other % TILE)
    )
    same[...] = one_hot(here == other)
    for half in range(2):
        at = section * 2 + half
        tt[half] = tiles_of([top_ref[half, :, pl.ds(j * LANES, LANES)] for j in range(TILE)])

        @pl.when(section == last)
        def _():
            pltpu.make_async_copy(tt.at[half], dy.at[at], dy_r.at[at]).start()

        @pl.when(section < last)
        def _():
            remote(tt.at[half], dy.at[at], tg_s.at[half], dy_r.at[at], last, me)

    wback[pl.ds(2 * inner, EXPERTS), :] = router_ref[...]
    wback[pl.ds(2 * inner + EXPERTS, LANES - EXPERTS), :] = jnp.zeros(
        (LANES - EXPERTS, width), jnp.bfloat16
    )
    for j in range(TILE):
        gt[pl.ds(j, 1), :] = gain_ref[:, pl.ds(j * LANES, LANES)].astype(jnp.float32)
    for e in range(EXPERTS):
        lane = lax.broadcasted_iota(jnp.int32, (PART, LANES), 1)
        place = lax.broadcasted_iota(jnp.int32, (PART, LANES), 0).astype(jnp.float32)
        pick[pl.ds(e * PART, PART), :] = jnp.where(
            lane == EXPERTS, -1.0 - place, jnp.where(lane == e, 1.0, 0.0)
        ).astype(jnp.bfloat16)
    ahead = jnp.where(section == last, 1, jnp.where(section == last - 1, 3, MICRO))

    @pl.loop(0, ahead + 1)
    def _(i):
        normed_step(i)

        @pl.when(i == 0)
        def _():
            for copy in weights:
                copy.wait()
            turn_weights()

    @pl.loop(0, MICRO + 1)
    def _(k):
        @pl.when(k < MICRO)
        def _():
            send_grad(k)

        normed_step(k + ahead + 1)

        @pl.when(k >= 1)
        def _():
            finish(k - 1)

        @pl.when(k < MICRO)
        def _():
            backward(k)

    @pl.loop(MICRO - 2, MICRO)
    def _(k):
        wait_bytes(xs.at[0, sent], xn_s.at[k])
        wait_bytes(ds.at[0, sent], d_s.at[k])

    @pl.loop(0, MICRO)
    def _(k):
        wait_bytes(xs.at[0, sent], c_s.at[k])

        @pl.when(section > 0)
        def _():
            wait_bytes(dy.at[0], dy_s.at[k])

    for half in range(2):

        @pl.when(section < last)
        def _():
            wait_bytes(dy.at[0], tg_s.at[half])


def shards(layer_inputs, top_grad, expert_ids, router, norm_gain, w_gate, w_up, w_down):
    width = layer_inputs.shape[3]
    inner = w_down.shape[2]
    vmem = pl.BlockSpec(memory_space=pltpu.VMEM)
    hbm = pl.BlockSpec(memory_space=pl.ANY)
    half = jnp.bfloat16
    tiles = (MICRO, ROWS, LANES)
    factor = (MICRO, SLOTS, inner)
    dma = pltpu.SemaphoreType.DMA
    out = pl.pallas_call(
        kernel,
        out_shape=jax.ShapeDtypeStruct((MICRO, OWN, LANES), half),
        in_specs=[vmem] * 5 + [hbm] * 3,
        out_specs=vmem,
        scratch_shapes=[
            pltpu.VMEM((width, 2 * inner), half),
            pltpu.VMEM((2 * inner + LANES, width), half),
            pltpu.VMEM((width, inner), half),
            pltpu.VMEM((256, 256), half),
            pltpu.VMEM((256, 256), half),
            pltpu.VMEM((MICRO, OWN, LANES), half),
            pltpu.VMEM((2, OWN, LANES), half),
            pltpu.VMEM((TILE, LANES), jnp.float32),
            pltpu.VMEM((ROWS, LANES), half),
            pltpu.VMEM((MICRO, OWN, LANES), half),
            pltpu.VMEM((MICRO, ROWS, OWN), half),
            pltpu.VMEM((2, OWN, ROWS), half),
            pltpu.VMEM((MICRO, OWN, LANES), half),
            pltpu.VMEM(tiles, half),
            pltpu.VMEM(tiles, half),
            pltpu.VMEM((2, ROWS, LANES), half),
            pltpu.VMEM((2, ROWS, LANES), half),
            pltpu.VMEM((SLOTS, width), half),
            pltpu.VMEM(factor, half),
            pltpu.VMEM(factor, half),
            pltpu.VMEM(factor, half),
            pltpu.VMEM((MICRO, SLOTS, LANES), jnp.float32),
            pltpu.VMEM((SLOTS, 2 * inner + LANES), half),
            dma((3,)),
        ]
        + [dma((MICRO,)) for _ in range(8)]
        + [dma((2,))],
        compiler_params=pltpu.CompilerParams(
            has_side_effects=True, vmem_limit_bytes=60 * 1024 * 1024
        ),
    )(
        layer_inputs[0],
        top_grad,
        jnp.transpose(expert_ids[0], (0, 2, 1)),
        norm_gain,
        jnp.transpose(router[0]),
        w_gate[0, 0],
        w_up[0, 0],
        w_down[0, 0],
    )
    return out.reshape(1, MICRO, TOK, width)


def solution(mesh):
    placed = (
        P("section", None, "expert", None),
        P("section", "expert", None),
        P("section", None, "expert", None),
        P("section", None, None),
        P("section", None),
        P("section", "expert", None, None),
        P("section", "expert", None, None),
        P("section", "expert", None, None),
    )
    return jax.shard_map(
        shards,
        mesh=mesh,
        in_specs=placed,
        out_specs=P("section", None, "expert", None),
        check_vma=False,
    )
```
